32 devices in a mesh: seg: 8 (over z, core), sec: 4 (over y, x).
Axes of the slice: x: 2, y: 2, z: 4, core: 2. Of those that a mesh axis runs over, the one named last changes fastest.
Arguments:
- psi_start: float32 [8, 4, 16, 128, 128], P('seg', 'sec'), may hold values from -6 to 6
- transfer: float32 [8, 4, 128, 128], P('seg', 'sec'), as said below
- coupling: float32 [4, 128, 128], P('sec'), may hold values from -0.5 to 0.5
- site_term: float32 [16, 16], replicated, may hold values from -1.5 to 1.5
- hop_out: float32 [4, 16], replicated, may hold values from -2 to 2
- hop_in: float32 [4, 16], replicated, may hold values from -2 to 2
- kept: int32 [8, 4], P('seg', 'sec'), may hold values from 32 to 128, as said below
Outputs:
- psi: float32 [8, 4, 16, 128, 128], P('seg', 'sec')
- energy: float32 [8], P('seg')
The draws below stay inside these ranges and needn't reach their ends.
Inputs may be any that keep to these rules, and one draw needn't show every extreme that they name: kept counts run from 32 to 128; some block keeps all 128 states. Each transfer block is the identity plus a full-rank perturbation of entries of order 0.3 / sqrt(128).
All inputs are finite; a program needn't handle non-finite values.
Results may differ from the reference program's by a relative error of at most 0.00035.
Values sent between devices are 32-bit elements; how exact they have to be, the bound alone decides.
A program may use at most 64 MiB of HBM per device.

```python
import jax
import jax.numpy as jnp
from jax import lax

SB = 128
NPH = 16
NHOP = 4
ITERS = 4
SEGS = 8
SECTORS = 4


def draw_transfer(key, part):
    key = jax.random.fold_in(key, 11)
    ident = jnp.eye(SB, dtype=jnp.float32)
    noise = 0.3 * jax.random.normal(key, (SEGS, SECTORS, SB, SB), jnp.float32)
    return ident[None, None, :, :] + noise / jnp.sqrt(jnp.float32(SB))


def draw_kept(key, part):
    key = jax.random.fold_in(key, 23)
    key_counts, key_place = jax.random.split(key)
    counts = jax.random.randint(key_counts, (SEGS * SECTORS,), SB // 4, SB + 1)
    place = jax.random.randint(key_place, (), 0, SEGS * SECTORS)
    counts = counts.at[place].set(SB)
    return counts.reshape(SEGS, SECTORS).astype(jnp.int32)


def block_levels(key, extent, pieces, smallest, top_value):
    gain, own = 1.0, jax.random.fold_in(key, 6)
    for axis_at, blocks in pieces:
        steps = jnp.exp(jax.random.uniform(jax.random.fold_in(own, axis_at), (blocks,), jnp.float32, smallest / len(pieces), top_value / len(pieces)))
        gain = gain * jnp.repeat(steps, extent[axis_at] // blocks).reshape([-1 if axis == axis_at else 1 for axis in range(len(extent))])
    return gain


def normal_values(key, dims, deviation, bound, cuts=(), held_as=jnp.bfloat16):
    level = block_levels(key, dims, cuts, -0.22, 0.18) if cuts else 1.0
    drawn = jax.random.normal(key, dims, jnp.float32) * deviation * level
    return jnp.minimum(jnp.maximum(drawn, -bound), bound).astype(held_as)


def setup_inputs(seed: int = 0) -> dict:
    seeds = jax.random.split(jax.random.key(seed), 8)
    psi_start = normal_values(seeds[0], (SEGS, SECTORS, NPH, SB, SB), 1.0, 6.0, ((0, 8), (1, 4)), jnp.float32)
    transfer = draw_transfer(jax.random.fold_in(seeds[7], 71), 0)
    coupling = normal_values(seeds[2], (SECTORS, SB, SB), SB ** -0.5, 0.5, ((0, 4),), jnp.float32)
    site_term = normal_values(seeds[3], (NPH, NPH), NPH ** -0.5, 1.5, (), jnp.float32)
    hop_out = normal_values(seeds[4], (NHOP, NPH), 0.3, 2.0, (), jnp.float32)
    hop_in = normal_values(seeds[5], (NHOP, NPH), 0.3, 2.0, (), jnp.float32)
    kept = draw_kept(jax.random.fold_in(seeds[7], 71), 0)
    return dict(psi_start=psi_start, transfer=transfer, coupling=coupling, site_term=site_term, hop_out=hop_out, hop_in=hop_in, kept=kept)


EPSILON = 1e-06
HIGH = lax.Precision.HIGHEST

def batched_product(first, second):
    return jnp.einsum('qij,qjk->qik', first, second, precision=HIGH)

def chain_envs(transfer):
    ident = jnp.broadcast_to(jnp.eye(SB, dtype=jnp.float32), (SECTORS, SB, SB))

    def forward(carry, matrix):
        return (batched_product(carry, matrix), carry)

    def backward(carry, matrix):
        return (batched_product(matrix, carry), carry)
    _, lefts = lax.scan(forward, ident, transfer)
    _, rights = lax.scan(backward, ident, transfer, reverse=True)
    left_env = jnp.einsum('sqji,sqjk->sqik', lefts, lefts, precision=HIGH)
    right_env = jnp.einsum('sqij,sqkj->sqik', rights, rights, precision=HIGH)
    return (left_env, right_env)

def reference(psi_start, transfer, coupling, site_term, hop_out, hop_in, kept):
    left_env, right_env = chain_envs(transfer)
    interaction = 0.5 * (site_term + site_term.T)
    keep = (jnp.arange(SB, dtype=jnp.int32)[None, None, :] < kept[:, :, None]).astype(jnp.float32)

    def solve(operands):
        start, left_seg, right_seg, keep_seg = operands
        mask = keep_seg[:, None, :, None] * keep_seg[:, None, None, :]

        def apply_hamiltonian(blocks):
            inner = jnp.einsum('qij,qpjk->qpik', left_seg, blocks, precision=HIGH)
            local = jnp.einsum('qpik,qkl->qpil', inner, right_seg, precision=HIGH)
            mixed = jnp.einsum('pr,qrij->qpij', interaction, blocks, precision=HIGH)
            lower = jnp.einsum('kp,qpij->qkij', hop_in, blocks, precision=HIGH)
            lower = jnp.concatenate([jnp.zeros_like(lower[:1]), lower[:-1]], axis=0)
            lower = jnp.einsum('qji,qkjl->qkil', coupling, lower, precision=HIGH)
            upper = jnp.einsum('kp,qpij->qkij', hop_out, blocks, precision=HIGH)
            upper = jnp.einsum('qij,qkjl->qkil', coupling, upper, precision=HIGH)
            upper = jnp.concatenate([upper[1:], jnp.zeros_like(upper[:1])], axis=0)
            hopping = jnp.einsum('kp,qkij->qpij', hop_out, lower, precision=HIGH)
            hopping = hopping + jnp.einsum('kp,qkij->qpij', hop_in, upper, precision=HIGH)
            return (local + mixed + hopping) * mask
        vector = start * mask
        vector = vector / jnp.sqrt(jnp.sum(vector * vector) + EPSILON)
        image = apply_hamiltonian(vector)
        lowest = jnp.float32(0.0)
        for iteration in range(ITERS):
            rayleigh = jnp.sum(vector * image)
            residual = image - rayleigh * vector
            res_norm = jnp.sqrt(jnp.sum(residual * residual) + EPSILON)
            search = residual / res_norm
            search_image = apply_hamiltonian(search)
            curvature = jnp.sum(search * search_image)
            half_gap = 0.5 * (curvature - rayleigh)
            lowest = 0.5 * (rayleigh + curvature) - jnp.sqrt(half_gap * half_gap + res_norm * res_norm)
            second = lowest - rayleigh
            scale = jnp.sqrt(res_norm * res_norm + second * second)
            vector = (res_norm * vector + second * search) / scale
            image = (res_norm * image + second * search_image) / scale
        return (vector, lowest)
    psi, energy = lax.map(solve, (psi_start, left_env, right_env, keep))
    return (psi, energy)
```

```python
import functools

import jax
import jax.numpy as jnp
from jax import lax
from jax.experimental import pallas as pl
from jax.experimental.pallas import tpu as pltpu
from jax.sharding import PartitionSpec as P

ITERS = 4
EPSILON = 1e-06
HIGH = lax.Precision.HIGHEST
MESH = pl.DeviceIdType.MESH
F32 = jnp.float32
BF16 = jnp.bfloat16
SUB = 8


def split(x):
    high = x.astype(BF16)
    return high, (x - high.astype(F32)).astype(BF16)


def dot(a, b):
    return jnp.dot(a, b, preferred_element_type=F32)


def dot3(a, b):
    return dot(a[0], b[0]) + (dot(a[0], b[1]) + dot(a[1], b[0]))


def exact(a, b):
    return jnp.dot(a, b, precision=HIGH, preferred_element_type=F32)


def exact_nt(a, b):
    return lax.dot_general(
        a, b, (((1,), (1,)), ((), ())), precision=HIGH, preferred_element_type=F32
    )


def spread(rows, columns):
    r = lax.broadcasted_iota(jnp.int32, (rows, columns), 0)
    c = lax.broadcasted_iota(jnp.int32, (rows, columns), 1)
    return jnp.where(lax.shift_right_logical(r, 3) == c, 1.0, 0.0).astype(F32)


def same_sub(rows, columns):
    r = lax.broadcasted_iota(jnp.int32, (rows, columns), 0)
    c = lax.broadcasted_iota(jnp.int32, (rows, columns), 1)
    return (r & 7) == (c & 7)


def lanes(ref_slice, count):
    groups, rows, n = ref_slice.shape
    return jnp.concatenate(
        [ref_slice[:, c * SUB:(c + 1) * SUB, :].reshape(groups * SUB, n) for c in range(count)],
        axis=1,
    )


def unlanes(value, count):
    rows, width = value.shape
    n = width // count
    return jnp.concatenate(
        [value[:, c * n:(c + 1) * n].reshape(rows // SUB, SUB, n) for c in range(count)],
        axis=1,
    )


def kernel(
    nseg, nsec,
    psi_ref, transfer_ref, coupling_ref, site_ref, hop_out_ref, hop_in_ref, kept_ref,
    out_ref, energy_ref,
    v_ref, w_ref, r_ref, u_ref, loc_ref, comp_ref, low_ref,
    send_up, send_down, recv_low, recv_high, dots_ref,
    mate_ref, chain_ref, left_ref, right_ref, coupt_ref,
    hopc_ref, hopo_ref, mix_ref, mixc_ref, mixo_ref,
    up_send, up_recv, down_send, down_recv, dot_send, dot_recv,
    mate_sems, chain_send, chain_recv,
):
    nph, sb, _ = psi_ref.shape
    nhop = hop_in_ref.shape[0]
    nchip = nseg // 2
    seg = lax.axis_index("seg")
    sec = lax.axis_index("sec")
    chip = lax.div(seg, 2)
    core = lax.rem(seg, 2)
    mate = chip * 2 + (1 - core)

    barrier = pltpu.get_barrier_semaphore()
    for d in range(1, nsec):
        pl.semaphore_signal(barrier, 1, device_id=(seg, lax.rem(sec + d, nsec)), device_id_type=MESH)
    pl.semaphore_signal(barrier, 1, device_id=(mate, sec), device_id_type=MESH)
    for d in range(1, nchip):
        other = lax.rem(chip + d, nchip) * 2 + core
        pl.semaphore_signal(barrier, 1, device_id=(other, sec), device_id_type=MESH)

    kept = kept_ref[0, 0]
    sub_iota = lax.broadcasted_iota(jnp.int32, (SUB, sb), 0)
    lane_keep = lax.broadcasted_iota(jnp.int32, (SUB, sb), 1) < kept
    chunk_count = sb // SUB

    def chunk_mask(rows, start):
        row = lax.broadcasted_iota(jnp.int32, (rows, sb), 0) + start
        col = lax.broadcasted_iota(jnp.int32, (rows, sb), 1)
        return jnp.where((row < kept) & (col < kept), 1.0, 0.0).astype(F32)

    hopc_ref[0:nhop, :] = hop_in_ref[...]
    hopc_ref[nhop:2 * nhop, :] = hop_out_ref[...]
    hopo_ref[0:nhop, :] = hop_out_ref[...]
    hopo_ref[nhop:2 * nhop, :] = hop_in_ref[...]
    e_ph = spread(nph * SUB, nph)
    e_hop = spread(2 * nhop * SUB, 2 * nhop)
    site = site_ref[...]
    half = 0.5 * (exact(e_ph, site) + exact_nt(e_ph, site))
    mix_ref[...] = jnp.where(same_sub(nph * SUB, nph * SUB), exact_nt(half, e_ph), 0.0)
    mixc_ref[...] = jnp.where(
        same_sub(2 * nhop * SUB, nph * SUB), exact_nt(exact(e_hop, hopc_ref[...]), e_ph), 0.0)
    mixo_ref[...] = jnp.where(
        same_sub(nph * SUB, 2 * nhop * SUB), exact_nt(exact_nt(e_ph, hopo_ref[...]), e_hop), 0.0)
    coupt_ref[...] = coupling_ref[...].T

    whole = chunk_mask(sb, 0)

    @pl.loop(0, nph)
    def _(p):
        v_ref[p] = psi_ref[p] * whole

    pl.semaphore_wait(barrier, (nsec - 1) + 1 + (nchip - 1))

    mate_copy = pltpu.make_async_remote_copy(
        src_ref=transfer_ref, dst_ref=mate_ref, send_sem=mate_sems.at[0],
        recv_sem=mate_sems.at[1], device_id=(mate, sec), device_id_type=MESH)
    mate_copy.start()

    @pl.when(sec == 0)
    def _():
        recv_low[...] = jnp.zeros_like(recv_low)

    @pl.when(sec == nsec - 1)
    def _():
        recv_high[...] = jnp.zeros_like(recv_high)

    up_to = jnp.minimum(sec + 1, nsec - 1)
    down_to = jnp.maximum(sec - 1, 0)

    def up_copy(e):
        return pltpu.make_async_remote_copy(
            src_ref=send_up.at[e], dst_ref=recv_low.at[e], send_sem=up_send.at[e],
            recv_sem=up_recv.at[e], device_id=(seg, up_to), device_id_type=MESH)

    def down_copy(e):
        return pltpu.make_async_remote_copy(
            src_ref=send_down.at[e], dst_ref=recv_high.at[e], send_sem=down_send.at[e],
            recv_sem=down_recv.at[e], device_id=(seg, down_to), device_id_type=MESH)

    def send_components(src, e):
        mats = split(mixc_ref[...])
        step = 4

        @pl.loop(0, chunk_count // step)
        def _(g):
            rows = pl.ds(pl.multiple_of(g * (step * SUB), step * SUB), step * SUB)
            parts = unlanes(dot3(mats, split(lanes(src[:, rows, :], step))), step)
            send_up[e, :, rows, :] = parts[:nhop]
            comp_ref[:, rows, :] = parts[nhop:]

        @pl.when(sec < nsec - 1)
        def _():
            up_copy(e).start()

        bond = split(coupling_ref[...])
        high = jnp.concatenate([comp_ref[k] for k in range(nhop)], axis=1)
        high = dot3(bond, split(high))
        for k in range(nhop):
            send_down[e, k] = high[:, k * sb:(k + 1) * sb]

        @pl.when(sec > 0)
        def _():
            down_copy(e).start()

    def local_part(src):
        right = split(right_ref[...])
        left = split(left_ref[...])
        group = 4

        @pl.loop(0, nph // group)
        def _(g):
            block = src[pl.ds(g * group, group)].reshape(group * sb, sb)
            inner = dot3(split(block), right)
            inner = jnp.concatenate([inner[k * sb:(k + 1) * sb] for k in range(group)], axis=1)
            inner = dot3(left, split(inner))
            for k in range(group):
                loc_ref[g * group + k] = inner[:, k * sb:(k + 1) * sb]

        mats = split(mix_ref[...])
        step = 2

        @pl.loop(0, chunk_count // step)
        def _(g):
            rows = pl.ds(pl.multiple_of(g * (step * SUB), step * SUB), step * SUB)
            loc_ref[:, rows, :] += unlanes(dot3(mats, split(lanes(src[:, rows, :], step))), step)

    def receive_components(e):
        @pl.when(sec > 0)
        def _():
            up_copy(e).wait_recv()

        low = jnp.concatenate([recv_low[e, k] for k in range(nhop)], axis=1)
        low = dot3(split(coupt_ref[...]), split(low))
        for k in range(nhop):
            low_ref[k] = low[:, k * sb:(k + 1) * sb]
        @pl.when(sec < nsec - 1)
        def _():
            down_copy(e).wait_recv()

    step = 2
    def over_chunks(e, ndots, update):
        mats = split(mixo_ref[...])

        def body(g, sums):
            start = pl.multiple_of(g * (step * SUB), step * SUB)
            rows = pl.ds(start, step * SUB)
            both = jnp.concatenate(
                [lanes(low_ref[:, rows, :], step), lanes(recv_high[e, :, rows, :], step)], axis=0)
            hopping = unlanes(dot3(mats, split(both)), step)
            image = (loc_ref[:, rows, :] + hopping) * chunk_mask(step * SUB, start)[None]
            return tuple(s + d for s, d in zip(sums, update(rows, image)))

        zero = jnp.zeros((SUB, sb), F32)
        return lax.fori_loop(0, chunk_count // step, body, (zero,) * ndots)

    def inner(a, b):
        prod = jnp.sum(a * b, axis=0)
        return jnp.sum(prod.reshape(step, SUB, sb), axis=0)

    def dot_copy(e, d):
        return pltpu.make_async_remote_copy(
            src_ref=dots_ref.at[e, sec], dst_ref=dots_ref.at[e, sec], send_sem=dot_send.at[e, d],
            recv_sem=dot_recv.at[e, d], device_id=(seg, lax.rem(sec + d, nsec)), device_id_type=MESH)

    def send_dots(e, parts):
        for n, part in enumerate(parts):
            dots_ref[e, sec, n] = part
        for d in range(1, nsec):
            dot_copy(e, d).start()

    def receive_dots(e, ndots):
        for d in range(1, nsec):
            dot_copy(e, d).wait_recv()
        totals = []
        for n in range(ndots):
            total = dots_ref[e, 0, n]
            for q in range(1, nsec):
                total = total + dots_ref[e, q, n]
            totals.append(jnp.sum(jnp.sum(total, axis=1, keepdims=True), axis=0, keepdims=True))
        return totals

    send_components(v_ref, 0)

    mate_copy.wait_recv()
    own, others = transfer_ref[...], mate_ref[...]
    first = jnp.where(core == 0, own, others)
    second = jnp.where(core == 0, others, own)

    chain_ref[chip] = exact(first, second)

    def chain_copy(d):
        other = lax.rem(chip + d, nchip) * 2 + core
        return pltpu.make_async_remote_copy(
            src_ref=chain_ref.at[chip], dst_ref=chain_ref.at[chip], send_sem=chain_send.at[d],
            recv_sem=chain_recv.at[d], device_id=(other, sec), device_id_type=MESH)

    for d in range(1, nchip):
        chain_copy(d).start()
    for d in range(1, nchip):
        chain_copy(d).wait_recv()
    r_i = lax.broadcasted_iota(jnp.int32, (sb, sb), 0)
    c_i = lax.broadcasted_iota(jnp.int32, (sb, sb), 1)
    ident = jnp.where(r_i == c_i, 1.0, 0.0).astype(F32)
    left = ident
    right = jnp.where(core == 0, second, ident)
    for c in range(nchip - 1):
        block = jnp.where(c < chip, chain_ref[c], ident)
        left = block if c == 0 else exact(left, block)
        right = exact(right, jnp.where(c + 1 > chip, chain_ref[c + 1], ident))
    left = exact(left, jnp.where(core == 1, first, ident))
    left_ref[...] = exact(left.T, left)
    right_ref[...] = exact_nt(right, right)

    local_part(v_ref)
    receive_components(0)

    def start_update(rows, image):
        w_ref[:, rows, :] = image
        v = v_ref[:, rows, :]
        return inner(v, v), inner(v, image)

    send_dots(0, over_chunks(0, 2, start_update))
    send_components(w_ref, 1)
    local_part(w_ref)
    norm2, raw = receive_dots(0, 2)
    inv = 1.0 / jnp.sqrt(norm2 + EPSILON)
    rayleigh = raw * (inv * inv)
    receive_components(1)

    def first_update(rows, image):
        v = v_ref[:, rows, :] * inv
        w = w_ref[:, rows, :] * inv
        r = w - rayleigh * v
        u = image * inv - rayleigh * w
        v_ref[:, rows, :] = v
        w_ref[:, rows, :] = w
        r_ref[:, rows, :] = r
        u_ref[:, rows, :] = u
        return inner(r, r), inner(r, u), inner(v, u), inner(r, w)

    send_dots(1, over_chunks(1, 4, first_update))

    def ritz(sums, rayleigh):
        rr, ru, vu, rw = sums
        square = rr + EPSILON
        res_norm = jnp.sqrt(square)
        curvature = ru / square
        half_gap = 0.5 * (curvature - rayleigh)
        lowest = 0.5 * (rayleigh + curvature) - jnp.sqrt(half_gap * half_gap + square)
        second = lowest - rayleigh
        scale = jnp.sqrt(square + second * second)
        a = res_norm / scale
        b = second / (res_norm * scale)
        following = a * a * rayleigh + a * b * (vu + rw) + b * b * ru
        return lowest, a, b, following

    for it in range(ITERS - 1):
        e = it + 2
        send_components(u_ref, e)
        local_part(u_ref)
        _, a, b, following = ritz(receive_dots(e - 1, 4), rayleigh)
        receive_components(e)
        previous = rayleigh

        def step_update(rows, image, a=a, b=b, following=following, previous=previous):
            v = v_ref[:, rows, :]
            w = w_ref[:, rows, :]
            u = u_ref[:, rows, :]
            v_new = a * v + b * r_ref[:, rows, :]
            w_new = a * w + b * u
            r_new = w_new - following * v_new
            u_new = a * (u + previous * w) + b * image - following * w_new
            v_ref[:, rows, :] = v_new
            w_ref[:, rows, :] = w_new
            r_ref[:, rows, :] = r_new
            u_ref[:, rows, :] = u_new
            return inner(r_new, r_new), inner(r_new, u_new), inner(v_new, u_new), inner(r_new, w_new)

        send_dots(e, over_chunks(e, 4, step_update))
        rayleigh = following

    lowest, a, b, _ = ritz(receive_dots(ITERS, 4), rayleigh)
    energy_ref[...] = lowest

    @pl.loop(0, nph)
    def _(p):
        out_ref[p] = a * v_ref[p] + b * r_ref[p]

    mate_copy.wait_send()
    for d in range(1, nchip):
        chain_copy(d).wait_send()
    for e in range(ITERS + 1):
        @pl.when(sec < nsec - 1)
        def _(e=e):
            up_copy(e).wait_send()

        @pl.when(sec > 0)
        def _(e=e):
            down_copy(e).wait_send()

        for d in range(1, nsec):
            dot_copy(e, d).wait_send()


def shards(nseg, nsec, psi_start, transfer, coupling, site_term, hop_out, hop_in, kept):
    _, _, nph, sb, _ = psi_start.shape
    nhop = hop_in.shape[0]
    rounds = ITERS + 1
    nchip = nseg // 2
    vmem = pl.BlockSpec(memory_space=pltpu.VMEM)
    smem = pl.BlockSpec(memory_space=pltpu.SMEM)
    block = pltpu.VMEM((nph, sb, sb), F32)
    parts = pltpu.VMEM((nhop, sb, sb), F32)
    sent = pltpu.VMEM((rounds, nhop, sb, sb), F32)
    square = pltpu.VMEM((sb, sb), F32)
    dma = pltpu.SemaphoreType.DMA
    psi, energy = pl.pallas_call(
        functools.partial(kernel, nseg, nsec),
        out_shape=(
            jax.ShapeDtypeStruct((nph, sb, sb), F32),
            jax.ShapeDtypeStruct((1, 1), F32),
        ),
        in_specs=[vmem] * 6 + [smem],
        out_specs=(vmem, vmem),
        scratch_shapes=[
            block, block, block, block, block, parts, parts,
            sent, sent, sent, sent,
            pltpu.VMEM((rounds, nsec, 4, SUB, sb), F32),
            square, pltpu.VMEM((nchip, sb, sb), F32), square, square, square,
            pltpu.VMEM((2 * nhop, nph), F32), pltpu.VMEM((2 * nhop, nph), F32),
            pltpu.VMEM((nph * SUB, nph * SUB), F32),
            pltpu.VMEM((2 * nhop * SUB, nph * SUB), F32),
            pltpu.VMEM((nph * SUB, 2 * nhop * SUB), F32),
            dma((rounds,)), dma((rounds,)), dma((rounds,)), dma((rounds,)),
            dma((rounds, nsec)), dma((rounds, nsec)),
            dma((2,)), dma((nchip,)), dma((nchip,)),
        ],
        compiler_params=pltpu.CompilerParams(
            collective_id=0, has_side_effects=True, vmem_limit_bytes=40 * 1024 * 1024
        ),
    )(psi_start[0, 0], transfer[0, 0], coupling[0], site_term, hop_out, hop_in, kept)
    return psi.reshape(psi_start.shape), energy.reshape(1)


def solution(mesh):
    placed = (
        P("seg", "sec", None, None, None),
        P("seg", "sec", None, None),
        P("sec", None, None),
        P(),
        P(),
        P(),
        P("seg", "sec"),
    )
    return jax.shard_map(
        functools.partial(shards, mesh.shape["seg"], mesh.shape["sec"]),
        mesh=mesh,
        in_specs=placed,
        out_specs=(P("seg", "sec", None, None, None), P("seg")),
        check_vma=False,
    )
```

```python
import functools

import jax
import jax.numpy as jnp
from jax import lax
from jax.experimental import pallas as pl
from jax.experimental.pallas import tpu as pltpu
from jax.sharding import PartitionSpec as P

ITERS = 4
EPSILON = 1e-06
HIGH = lax.Precision.HIGHEST
MESH = pl.DeviceIdType.MESH
F32 = jnp.float32
BF16 = jnp.bfloat16
SUB = 8


def split(x):
    high = x.astype(BF16)
    return high, (x - high.astype(F32)).astype(BF16)


def dot(a, b):
    return jnp.dot(a, b, preferred_element_type=F32)


def dot3(a, b):
    return dot(a[0], b[0]) + (dot(a[0], b[1]) + dot(a[1], b[0]))


def exact(a, b):
    return jnp.dot(a, b, precision=HIGH, preferred_element_type=F32)


def exact_nt(a, b):
    return lax.dot_general(
        a, b, (((1,), (1,)), ((), ())), precision=HIGH, preferred_element_type=F32
    )


def spread(rows, columns):
    r = lax.broadcasted_iota(jnp.int32, (rows, columns), 0)
    c = lax.broadcasted_iota(jnp.int32, (rows, columns), 1)
    return jnp.where(lax.shift_right_logical(r, 3) == c, 1.0, 0.0).astype(F32)


def same_sub(rows, columns):
    r = lax.broadcasted_iota(jnp.int32, (rows, columns), 0)
    c = lax.broadcasted_iota(jnp.int32, (rows, columns), 1)
    return (r & 7) == (c & 7)


def lanes(ref_slice, count):
    groups, rows, n = ref_slice.shape
    return jnp.concatenate(
        [ref_slice[:, c * SUB:(c + 1) * SUB, :].reshape(groups * SUB, n) for c in range(count)],
        axis=1,
    )


def unlanes(value, count):
    rows, width = value.shape
    n = width // count
    return jnp.concatenate(
        [value[:, c * n:(c + 1) * n].reshape(rows // SUB, SUB, n) for c in range(count)],
        axis=1,
    )


def kernel(
    nseg, nsec,
    psi_ref, transfer_ref, bond_ref, site_ref, hop_out_ref, hop_in_ref, kept_ref,
    out_ref, energy_ref,
    v_ref, w_ref, r_ref, u_ref, loc_ref, comp_ref, low_ref,
    send_up, send_down, recv_low, recv_high, dots_ref,
    pair_ref, chain_ref, left_ref, right_ref, coupt_ref, coupling_ref,
    hopc_ref, hopo_ref, mix_ref, mixc_ref, mixo_ref,
    keep_own, keep_ref, energy_own, energy_got,
    up_send, up_recv, down_send, down_recv, dot_send, dot_recv,
    chain_send, chain_recv, pair_send, pair_recv, swap_send, swap_recv,
    out_send, out_recv,
):
    nph, sb, _ = psi_ref.shape
    nhop = hop_in_ref.shape[0]
    nchip = nseg // 2
    home_seg = lax.axis_index("seg")
    home_sec = lax.axis_index("sec")
    chip = lax.div(home_seg, 2)
    core = lax.rem(home_seg, 2)
    pair = lax.div(home_sec, 2)
    side = lax.rem(home_sec, 2)
    sec = pair * 2 + core
    partner = (chip * 2 + side, pair * 2 + core)

    def at_sector(q):
        return (chip * 2 + lax.rem(q, 2), lax.div(q, 2) * 2 + side)

    def at_chip(c):
        return (c * 2 + core, home_sec)

    barrier = pltpu.get_barrier_semaphore()

    def greet(device):
        pl.semaphore_signal(barrier, 1, device_id=device, device_id_type=MESH)

    for dc, ds in ((0, 1), (1, 0), (1, 1)):
        greet((chip * 2 + lax.rem(core + dc, 2), pair * 2 + lax.rem(side + ds, 2)))
    for d in range(1, nsec // 2):
        other = lax.rem(pair + d, nsec // 2) * 2
        for k in range(2):
            greet((chip * 2 + k, other + side))
    for d in range(1, nchip):
        greet(at_chip(lax.rem(chip + d, nchip)))

    chunk_count = sb // SUB
    keep_own[...] = jnp.full((SUB, sb), kept_ref[0, 0].astype(F32), F32)

    def chunk_mask(rows, start):
        row = lax.broadcasted_iota(jnp.int32, (rows, sb), 0) + start
        col = lax.broadcasted_iota(jnp.int32, (rows, sb), 1)
        kept = keep_ref[0:1, 0:1]
        inside = (row.astype(F32) < kept) & (col.astype(F32) < kept)
        return jnp.where(inside, 1.0, 0.0).astype(F32)

    hopc_ref[0:nhop, :] = hop_in_ref[...]
    hopc_ref[nhop:2 * nhop, :] = hop_out_ref[...]
    hopo_ref[0:nhop, :] = hop_out_ref[...]
    hopo_ref[nhop:2 * nhop, :] = hop_in_ref[...]
    e_ph = spread(nph * SUB, nph)
    e_hop = spread(2 * nhop * SUB, 2 * nhop)
    site = site_ref[...]
    half = 0.5 * (exact(e_ph, site) + exact_nt(e_ph, site))
    mix_ref[...] = jnp.where(same_sub(nph * SUB, nph * SUB), exact_nt(half, e_ph), 0.0)
    mixc_ref[...] = jnp.where(
        same_sub(2 * nhop * SUB, nph * SUB), exact_nt(exact(e_hop, hopc_ref[...]), e_ph), 0.0)
    mixo_ref[...] = jnp.where(
        same_sub(nph * SUB, 2 * nhop * SUB), exact_nt(exact_nt(e_ph, hopo_ref[...]), e_hop), 0.0)

    pl.semaphore_wait(barrier, 3 + (nsec - 2) + (nchip - 1))

    def pair_local():
        return pltpu.make_async_copy(transfer_ref, pair_ref.at[core], pair_recv.at[core])

    def pair_remote(k, slot):
        return pltpu.make_async_remote_copy(
            src_ref=transfer_ref, dst_ref=pair_ref.at[slot], send_sem=pair_send.at[k],
            recv_sem=pair_recv.at[slot], device_id=(chip * 2 + side, pair * 2 + k),
            device_id_type=MESH)

    stays = core == side
    moved = core != side

    for k in range(2):
        @pl.when(jnp.logical_not(stays & (side == k)))
        def _(k=k):
            pair_remote(k, core).start()

    @pl.when(stays)
    def _():
        pair_local().start()

    items = ((psi_ref, v_ref), (bond_ref, coupling_ref), (keep_own, keep_ref))

    def swap_local(n):
        return pltpu.make_async_copy(items[n][0], items[n][1], swap_recv.at[n])

    def swap_remote(n):
        return pltpu.make_async_remote_copy(
            src_ref=items[n][0], dst_ref=items[n][1], send_sem=swap_send.at[n],
            recv_sem=swap_recv.at[n], device_id=partner, device_id_type=MESH)

    @pl.when(stays)
    def _():
        for n in (2, 1, 0):
            swap_local(n).start()

    @pl.when(moved)
    def _():
        for n in (2, 1, 0):
            swap_remote(n).start()

    @pl.when(sec == 0)
    def _():
        recv_low[...] = jnp.zeros_like(recv_low)

    @pl.when(sec == nsec - 1)
    def _():
        recv_high[...] = jnp.zeros_like(recv_high)

    up_to = at_sector(jnp.minimum(sec + 1, nsec - 1))
    down_to = at_sector(jnp.maximum(sec - 1, 0))
    hh = nhop // 2

    def up_copy(e):
        part = pl.ds(0, hh if e == ITERS else nhop)
        return pltpu.make_async_remote_copy(
            src_ref=send_up.at[e, part], dst_ref=recv_low.at[e, part], send_sem=up_send.at[e],
            recv_sem=up_recv.at[e], device_id=up_to, device_id_type=MESH)

    def down_copy(e):
        part = pl.ds(hh, nhop - hh) if e == ITERS else pl.ds(0, nhop)
        return pltpu.make_async_remote_copy(
            src_ref=send_down.at[e, part], dst_ref=recv_high.at[e, part], send_sem=down_send.at[e],
            recv_sem=down_recv.at[e], device_id=down_to, device_id_type=MESH)

    def send_components(src, e):
        mats = split(mixc_ref[...])
        step = 4

        for g in range(chunk_count // step):
            rows = pl.ds(g * (step * SUB), step * SUB)
            parts = unlanes(dot3(mats, split(lanes(src[:, rows, :], step))), step)
            send_up[e, :, rows, :] = parts[:nhop]
            comp_ref[:, rows, :] = parts[nhop:]

        @pl.when(sec < nsec - 1)
        def _():
            up_copy(e).start()

        bond = split(coupling_ref[...])
        which = range(hh if e == ITERS else 0, nhop)
        high = jnp.concatenate([comp_ref[k] for k in which], axis=1)
        high = dot3(bond, split(high))
        for n, k in enumerate(which):
            send_down[e, k] = high[:, n * sb:(n + 1) * sb]

        @pl.when(sec > 0)
        def _():
            down_copy(e).start()

    def local_part(src):
        right = split(right_ref[...])
        left = split(left_ref[...])
        group = 4

        for g in range(nph // group):
            block = src[pl.ds(g * group, group)].reshape(group * sb, sb)
            inner = dot3(split(block), right)
            inner = jnp.concatenate([inner[k * sb:(k + 1) * sb] for k in range(group)], axis=1)
            inner = dot3(left, split(inner))
            for k in range(group):
                loc_ref[g * group + k] = inner[:, k * sb:(k + 1) * sb]

        mats = split(mix_ref[...])
        step = 4
        for g in range(chunk_count // step):
            rows = pl.ds(g * (step * SUB), step * SUB)
            loc_ref[:, rows, :] += unlanes(dot3(mats, split(lanes(src[:, rows, :], step))), step)

    def await_components(e):
        @pl.when(sec > 0)
        def _():
            up_copy(e).wait_recv()

        @pl.when(sec < nsec - 1)
        def _():
            down_copy(e).wait_recv()

    def bond_product(e, count):
        low = jnp.concatenate([recv_low[e, k] for k in range(count)], axis=1)
        return dot3(split(coupt_ref[...]), split(low))

    def receive_components(e):
        await_components(e)
        low = bond_product(e, nhop)
        for k in range(nhop):
            low_ref[k] = low[:, k * sb:(k + 1) * sb]

    step = 2

    def over_chunks(e, ndots, update):
        mats = split(mixo_ref[...])
        sums = (jnp.zeros((SUB, sb), F32),) * ndots
        for g in range(chunk_count // step):
            rows = pl.ds(g * (step * SUB), step * SUB)
            both = jnp.concatenate(
                [lanes(low_ref[:, rows, :], step), lanes(recv_high[e, :, rows, :], step)], axis=0)
            hopping = unlanes(dot3(mats, split(both)), step)
            mask = chunk_mask(step * SUB, g * step * SUB)[None]
            image = (loc_ref[:, rows, :] + hopping) * mask
            sums = tuple(s + d for s, d in zip(sums, update(rows, image)))
        return sums

    def inner(a, b):
        prod = jnp.sum(a * b, axis=0)
        return jnp.sum(prod.reshape(step, SUB, sb), axis=0)

    def dot_copy(e, d):
        return pltpu.make_async_remote_copy(
            src_ref=dots_ref.at[e, sec], dst_ref=dots_ref.at[e, sec], send_sem=dot_send.at[e, d],
            recv_sem=dot_recv.at[e, d], device_id=at_sector(lax.rem(sec + d, nsec)), device_id_type=MESH)

    def send_dots(e, parts):
        for n, part in enumerate(parts):
            dots_ref[e, sec, n] = part
        for d in range(1, nsec):
            dot_copy(e, d).start()

    def receive_dots(e, ndots):
        for d in range(1, nsec):
            dot_copy(e, d).wait_recv()
        totals = []
        for n in range(ndots):
            total = dots_ref[e, 0, n]
            for q in range(1, nsec):
                total = total + dots_ref[e, q, n]
            totals.append(jnp.sum(jnp.sum(total, axis=1, keepdims=True), axis=0, keepdims=True))
        return totals

    for g in range(2):
        @pl.when(stays & (core == g))
        def _(g=g):
            pair_local().wait()

        @pl.when(jnp.logical_not(stays & (core == g)))
        def _(g=g):
            pair_remote(0, g).wait_recv()
    first, second = pair_ref[0], pair_ref[1]
    chain_ref[chip] = exact(first, second)

    def chain_copy(d):
        return pltpu.make_async_remote_copy(
            src_ref=chain_ref.at[chip], dst_ref=chain_ref.at[chip], send_sem=chain_send.at[d],
            recv_sem=chain_recv.at[d], device_id=at_chip(lax.rem(chip + d, nchip)), device_id_type=MESH)

    for d in range(1, nchip):
        chain_copy(d).start()

    for n in (2, 1, 0):
        @pl.when(stays)
        def _(n=n):
            swap_local(n).wait()

        @pl.when(moved)
        def _(n=n):
            swap_remote(n).wait_recv()

    coupt_ref[...] = coupling_ref[...].T
    whole = chunk_mask(sb, 0)
    for p in range(nph):
        v_ref[p] = v_ref[p] * whole
    send_components(v_ref, 0)

    for d in range(1, nchip):
        chain_copy(d).wait_recv()
    r_i = lax.broadcasted_iota(jnp.int32, (sb, sb), 0)
    c_i = lax.broadcasted_iota(jnp.int32, (sb, sb), 1)
    ident = jnp.where(r_i == c_i, 1.0, 0.0).astype(F32)
    left = ident
    right = jnp.where(side == 0, second, ident)
    for c in range(nchip - 1):
        block = jnp.where(c < chip, chain_ref[c], ident)
        left = block if c == 0 else exact(left, block)
        right = exact(right, jnp.where(c + 1 > chip, chain_ref[c + 1], ident))
    left = exact(left, jnp.where(side == 1, first, ident))
    left_ref[...] = exact(left.T, left)
    right_ref[...] = exact_nt(right, right)

    local_part(v_ref)
    receive_components(0)

    def start_update(rows, image):
        w_ref[:, rows, :] = image
        v = v_ref[:, rows, :]
        return inner(v, v), inner(v, image)

    send_dots(0, over_chunks(0, 2, start_update))
    send_components(w_ref, 1)
    local_part(w_ref)
    norm2, raw = receive_dots(0, 2)
    inv = 1.0 / jnp.sqrt(norm2 + EPSILON)
    rayleigh = raw * (inv * inv)
    receive_components(1)

    def first_update(rows, image):
        v = v_ref[:, rows, :] * inv
        w = w_ref[:, rows, :] * inv
        r = w - rayleigh * v
        u = image * inv - rayleigh * w
        v_ref[:, rows, :] = v
        w_ref[:, rows, :] = w
        r_ref[:, rows, :] = r
        u_ref[:, rows, :] = u
        return inner(r, r), inner(r, u), inner(v, u), inner(r, w)

    send_dots(1, over_chunks(1, 4, first_update))

    def ritz(sums, rayleigh):
        rr, ru, vu, rw = sums
        square = rr + EPSILON
        res_norm = jnp.sqrt(square)
        curvature = ru / square
        half_gap = 0.5 * (curvature - rayleigh)
        lowest = 0.5 * (rayleigh + curvature) - jnp.sqrt(half_gap * half_gap + square)
        second = lowest - rayleigh
        scale = jnp.sqrt(square + second * second)
        a = res_norm / scale
        b = second / (res_norm * scale)
        following = a * a * rayleigh + a * b * (vu + rw) + b * b * ru
        return lowest, a, b, following

    for it in range(ITERS - 2):
        e = it + 2
        send_components(u_ref, e)
        local_part(u_ref)
        _, a, b, following = ritz(receive_dots(e - 1, 4), rayleigh)
        receive_components(e)
        previous = rayleigh

        def step_update(rows, image, a=a, b=b, following=following, previous=previous):
            v = v_ref[:, rows, :]
            w = w_ref[:, rows, :]
            u = u_ref[:, rows, :]
            v_new = a * v + b * r_ref[:, rows, :]
            w_new = a * w + b * u
            r_new = w_new - following * v_new
            u_new = a * (u + previous * w) + b * image - following * w_new
            v_ref[:, rows, :] = v_new
            w_ref[:, rows, :] = w_new
            r_ref[:, rows, :] = r_new
            u_ref[:, rows, :] = u_new
            return inner(r_new, r_new), inner(r_new, u_new), inner(v_new, u_new), inner(r_new, w_new)

        send_dots(e, over_chunks(e, 4, step_update))
        rayleigh = following

    e = ITERS
    send_components(u_ref, e)
    local_part(u_ref)
    _, a, b, following = ritz(receive_dots(e - 1, 4), rayleigh)
    square = jnp.zeros((SUB, sb), F32)
    image_sum = jnp.zeros((SUB, sb), F32)
    for g in range(chunk_count // step):
        rows = pl.ds(g * (step * SUB), step * SUB)
        v = v_ref[:, rows, :]
        w = w_ref[:, rows, :]
        u = u_ref[:, rows, :]
        v_new = a * v + b * r_ref[:, rows, :]
        w_new = a * w + b * u
        r_new = w_new - following * v_new
        known = u + rayleigh * w
        v_ref[:, rows, :] = v_new
        r_ref[:, rows, :] = r_new
        square = square + inner(r_new, r_new)
        image_sum = image_sum + inner(r_new, a * known - following * w_new)
        image_sum = image_sum + b * inner(
            u, a * known + b * loc_ref[:, rows, :] - following * w_new)

    await_components(e)
    low = bond_product(e, hh)
    twice = jnp.zeros((sb, sb), F32)
    for k in range(hh):
        twice = twice + low[:, k * sb:(k + 1) * sb] * comp_ref[k]
    for k in range(hh, nhop):
        twice = twice + recv_high[e, k] * send_up[e, k]
    twice = jnp.sum(twice.reshape(chunk_count, SUB, sb), axis=0)
    send_dots(e, (square, image_sum + (2.0 * b * b) * twice))
    rr, ru = receive_dots(e, 2)
    zero = jnp.zeros((1, 1), F32)
    lowest, a, b, _ = ritz((rr, ru, zero, zero), following)
    energy_own[...] = jnp.broadcast_to(lowest, (SUB, sb))

    nout = 4
    per = nph // nout

    def out_local(n):
        part = pl.ds(n * per, per)
        return pltpu.make_async_copy(w_ref.at[part], out_ref.at[part], out_recv.at[n])

    def out_remote(n):
        part = pl.ds(n * per, per)
        return pltpu.make_async_remote_copy(
            src_ref=w_ref.at[part], dst_ref=out_ref.at[part], send_sem=out_send.at[n],
            recv_sem=out_recv.at[n], device_id=partner, device_id_type=MESH)

    def energy_remote():
        return pltpu.make_async_remote_copy(
            src_ref=energy_own, dst_ref=energy_got, send_sem=out_send.at[nout],
            recv_sem=out_recv.at[nout], device_id=partner, device_id_type=MESH)

    @pl.when(moved)
    def _():
        energy_remote().start()

    @pl.when(stays)
    def _():
        energy_got[...] = energy_own[...]

    for n in range(nout):
        for p in range(n * per, (n + 1) * per):
            w_ref[p] = a * v_ref[p] + b * r_ref[p]

        @pl.when(moved)
        def _(n=n):
            out_remote(n).start()

        @pl.when(stays)
        def _(n=n):
            out_local(n).start()

    @pl.when(moved)
    def _():
        energy_remote().wait()
        for n in range(nout):
            out_remote(n).wait()
        for n in range(3):
            swap_remote(n).wait_send()

    @pl.when(stays)
    def _():
        for n in range(nout):
            out_local(n).wait()

    energy_ref[...] = energy_got[0:1, 0:1]

    for k in range(2):
        @pl.when(jnp.logical_not(stays & (side == k)))
        def _(k=k):
            pair_remote(k, core).wait_send()

    for d in range(1, nchip):
        chain_copy(d).wait_send()
    for e in range(ITERS + 1):
        @pl.when(sec < nsec - 1)
        def _(e=e):
            up_copy(e).wait_send()

        @pl.when(sec > 0)
        def _(e=e):
            down_copy(e).wait_send()

        for d in range(1, nsec):
            dot_copy(e, d).wait_send()


def shards(nseg, nsec, psi_start, transfer, coupling, site_term, hop_out, hop_in, kept):
    _, _, nph, sb, _ = psi_start.shape
    nhop = hop_in.shape[0]
    rounds = ITERS + 1
    nchip = nseg // 2
    vmem = pl.BlockSpec(memory_space=pltpu.VMEM)
    anywhere = pl.BlockSpec(memory_space=pl.ANY)
    smem = pl.BlockSpec(memory_space=pltpu.SMEM)
    block = pltpu.VMEM((nph, sb, sb), F32)
    parts = pltpu.VMEM((nhop, sb, sb), F32)
    sent = pltpu.VMEM((rounds, nhop, sb, sb), F32)
    square = pltpu.VMEM((sb, sb), F32)
    tile = pltpu.VMEM((SUB, sb), F32)
    dma = pltpu.SemaphoreType.DMA
    psi, energy = pl.pallas_call(
        functools.partial(kernel, nseg, nsec),
        out_shape=(
            jax.ShapeDtypeStruct((nph, sb, sb), F32),
            jax.ShapeDtypeStruct((1, 1), F32),
        ),
        in_specs=[anywhere] * 3 + [vmem] * 3 + [smem],
        out_specs=(anywhere, vmem),
        scratch_shapes=[
            block, block, block, block, block, parts, parts,
            sent, sent, sent, sent,
            pltpu.VMEM((rounds, nsec, 4, SUB, sb), F32),
            pltpu.VMEM((2, sb, sb), F32), pltpu.VMEM((nchip, sb, sb), F32),
            square, square, square, square,
            pltpu.VMEM((2 * nhop, nph), F32), pltpu.VMEM((2 * nhop, nph), F32),
            pltpu.VMEM((nph * SUB, nph * SUB), F32),
            pltpu.VMEM((2 * nhop * SUB, nph * SUB), F32),
            pltpu.VMEM((nph * SUB, 2 * nhop * SUB), F32),
            tile, tile, tile, tile,
            dma((rounds,)), dma((rounds,)), dma((rounds,)), dma((rounds,)),
            dma((rounds, nsec)), dma((rounds, nsec)),
            dma((nchip,)), dma((nchip,)), dma((2,)), dma((2,)), dma((3,)), dma((3,)),
            dma((5,)), dma((5,)),
        ],
        compiler_params=pltpu.CompilerParams(
            collective_id=0, has_side_effects=True, vmem_limit_bytes=40 * 1024 * 1024
        ),
    )(psi_start[0, 0], transfer[0, 0], coupling[0], site_term, hop_out, hop_in, kept)
    return psi.reshape(psi_start.shape), energy.reshape(1)


def solution(mesh):
    placed = (
        P("seg", "sec", None, None, None),
        P("seg", "sec", None, None),
        P("sec", None, None),
        P(),
        P(),
        P(),
        P("seg", "sec"),
    )
    return jax.shard_map(
        functools.partial(shards, mesh.shape["seg"], mesh.shape["sec"]),
        mesh=mesh,
        in_specs=placed,
        out_specs=(P("seg", "sec", None, None, None), P("seg")),
        check_vma=False,
    )
```

```python
import functools

import jax
import jax.numpy as jnp
from jax import lax
from jax.experimental import pallas as pl
from jax.experimental.pallas import tpu as pltpu
from jax.sharding import PartitionSpec as P

ITERS = 4
EPSILON = 1e-06
HIGH = lax.Precision.HIGHEST
MESH = pl.DeviceIdType.MESH
F32 = jnp.float32
BF16 = jnp.bfloat16
SUB = 8


def split(x):
    high = x.astype(BF16)
    return high, (x - high.astype(F32)).astype(BF16)


def dot(a, b):
    return jnp.dot(a, b, preferred_element_type=F32)


def dot3(a, b):
    return dot(a[0], b[0]) + (dot(a[0], b[1]) + dot(a[1], b[0]))


def exact(a, b):
    return jnp.dot(a, b, precision=HIGH, preferred_element_type=F32)


def exact_nt(a, b):
    return lax.dot_general(
        a, b, (((1,), (1,)), ((), ())), precision=HIGH, preferred_element_type=F32
    )


def spread(rows, columns):
    r = lax.broadcasted_iota(jnp.int32, (rows, columns), 0)
    c = lax.broadcasted_iota(jnp.int32, (rows, columns), 1)
    return jnp.where(lax.shift_right_logical(r, 3) == c, 1.0, 0.0).astype(F32)


def same_sub(rows, columns):
    r = lax.broadcasted_iota(jnp.int32, (rows, columns), 0)
    c = lax.broadcasted_iota(jnp.int32, (rows, columns), 1)
    return (r & 7) == (c & 7)


def lanes(ref_slice, count):
    groups, rows, n = ref_slice.shape
    return jnp.concatenate(
        [ref_slice[:, c * SUB:(c + 1) * SUB, :].reshape(groups * SUB, n) for c in range(count)],
        axis=1,
    )


def unlanes(value, count):
    rows, width = value.shape
    n = width // count
    return jnp.concatenate(
        [value[:, c * n:(c + 1) * n].reshape(rows // SUB, SUB, n) for c in range(count)],
        axis=1,
    )


def kernel(
    nseg, nsec,
    psi_ref, transfer_ref, bond_ref, site_ref, hop_out_ref, hop_in_ref, kept_ref,
    out_ref, energy_ref,
    v_ref, w_ref, r_ref, u_ref, loc_ref, comp_ref, low_ref,
    send_up, send_down, recv_low, recv_high, dots_ref,
    pair_ref, chain_ref, left_ref, right_ref, coupt_ref, coupling_ref,
    hopc_ref, hopo_ref, mix_ref, mixc_ref, mixo_ref,
    keep_own, keep_ref, energy_own, energy_got,
    up_send, up_recv, down_send, down_recv, dot_send, dot_recv,
    chain_send, chain_recv, pair_send, pair_recv, swap_send, swap_recv,
    out_send, out_recv,
):
    nph, sb, _ = psi_ref.shape
    nhop = hop_in_ref.shape[0]
    nchip = nseg // 2
    home_seg = lax.axis_index("seg")
    home_sec = lax.axis_index("sec")
    chip = lax.div(home_seg, 2)
    core = lax.rem(home_seg, 2)
    pair = lax.div(home_sec, 2)
    side = lax.rem(home_sec, 2)
    sec = pair * 2 + core
    partner = (chip * 2 + side, pair * 2 + core)

    def at_sector(q):
        return (chip * 2 + lax.rem(q, 2), lax.div(q, 2) * 2 + side)

    def at_chip(c):
        return (c * 2 + core, home_sec)

    barrier = pltpu.get_barrier_semaphore()

    def greet(device):
        pl.semaphore_signal(barrier, 1, device_id=device, device_id_type=MESH)

    for dc, ds in ((0, 1), (1, 0), (1, 1)):
        greet((chip * 2 + lax.rem(core + dc, 2), pair * 2 + lax.rem(side + ds, 2)))
    for d in range(1, nsec // 2):
        other = lax.rem(pair + d, nsec // 2) * 2
        for k in range(2):
            greet((chip * 2 + k, other + side))
    for d in range(1, nchip):
        greet(at_chip(lax.rem(chip + d, nchip)))

    chunk_count = sb // SUB
    keep_own[...] = jnp.full((SUB, sb), kept_ref[0, 0].astype(F32), F32)

    def chunk_mask(rows, start):
        row = lax.broadcasted_iota(jnp.int32, (rows, sb), 0) + start
        col = lax.broadcasted_iota(jnp.int32, (rows, sb), 1)
        kept = keep_ref[0:1, 0:1]
        inside = (row.astype(F32) < kept) & (col.astype(F32) < kept)
        return jnp.where(inside, 1.0, 0.0).astype(F32)

    hopc_ref[0:nhop, :] = hop_in_ref[...]
    hopc_ref[nhop:2 * nhop, :] = hop_out_ref[...]
    hopo_ref[0:nhop, :] = hop_out_ref[...]
    hopo_ref[nhop:2 * nhop, :] = hop_in_ref[...]
    e_ph = spread(nph * SUB, nph)
    e_hop = spread(2 * nhop * SUB, 2 * nhop)
    site = site_ref[...]
    half = 0.5 * (exact(e_ph, site) + exact_nt(e_ph, site))
    mix_ref[...] = jnp.where(same_sub(nph * SUB, nph * SUB), exact_nt(half, e_ph), 0.0)
    mixc_ref[...] = jnp.where(
        same_sub(2 * nhop * SUB, nph * SUB), exact_nt(exact(e_hop, hopc_ref[...]), e_ph), 0.0)
    mixo_ref[...] = jnp.where(
        same_sub(nph * SUB, 2 * nhop * SUB), exact_nt(exact_nt(e_ph, hopo_ref[...]), e_hop), 0.0)

    pl.semaphore_wait(barrier, 3 + (nsec - 2) + (nchip - 1))

    def pair_local():
        return pltpu.make_async_copy(transfer_ref, pair_ref.at[core], pair_recv.at[core])

    def pair_remote(k, slot):
        return pltpu.make_async_remote_copy(
            src_ref=transfer_ref, dst_ref=pair_ref.at[slot], send_sem=pair_send.at[k],
            recv_sem=pair_recv.at[slot], device_id=(chip * 2 + side, pair * 2 + k),
            device_id_type=MESH)

    stays = core == side
    moved = core != side

    for k in range(2):
        @pl.when(jnp.logical_not(stays & (side == k)))
        def _(k=k):
            pair_remote(k, core).start()

    @pl.when(stays)
    def _():
        pair_local().start()

    items = ((psi_ref, v_ref), (bond_ref, coupling_ref), (keep_own, keep_ref))

    def swap_local(n):
        return pltpu.make_async_copy(items[n][0], items[n][1], swap_recv.at[n])

    def swap_remote(n):
        return pltpu.make_async_remote_copy(
            src_ref=items[n][0], dst_ref=items[n][1], send_sem=swap_send.at[n],
            recv_sem=swap_recv.at[n], device_id=partner, device_id_type=MESH)

    @pl.when(stays)
    def _():
        for n in (2, 1, 0):
            swap_local(n).start()

    @pl.when(moved)
    def _():
        for n in (2, 1, 0):
            swap_remote(n).start()

    @pl.when(sec == 0)
    def _():
        recv_low[...] = jnp.zeros_like(recv_low)

    @pl.when(sec == nsec - 1)
    def _():
        recv_high[...] = jnp.zeros_like(recv_high)

    up_to = at_sector(jnp.minimum(sec + 1, nsec - 1))
    down_to = at_sector(jnp.maximum(sec - 1, 0))
    hh = nhop // 2

    def up_copy(e):
        part = pl.ds(0, hh if e == ITERS else nhop)
        return pltpu.make_async_remote_copy(
            src_ref=send_up.at[e, part], dst_ref=recv_low.at[e, part], send_sem=up_send.at[e],
            recv_sem=up_recv.at[e], device_id=up_to, device_id_type=MESH)

    def down_copy(e):
        part = pl.ds(hh, nhop - hh) if e == ITERS else pl.ds(0, nhop)
        return pltpu.make_async_remote_copy(
            src_ref=send_down.at[e, part], dst_ref=recv_high.at[e, part], send_sem=down_send.at[e],
            recv_sem=down_recv.at[e], device_id=down_to, device_id_type=MESH)

    def send_components(src, e):
        mats = split(mixc_ref[...])
        step = 4

        for g in range(chunk_count // step):
            rows = pl.ds(g * (step * SUB), step * SUB)
            parts = unlanes(dot3(mats, split(lanes(src[:, rows, :], step))), step)
            send_up[e, :, rows, :] = parts[:nhop]
            comp_ref[:, rows, :] = parts[nhop:]

        @pl.when(sec < nsec - 1)
        def _():
            up_copy(e).start()

        bond = split(coupling_ref[...])
        which = range(hh if e == ITERS else 0, nhop)
        high = jnp.concatenate([comp_ref[k] for k in which], axis=1)
        high = dot3(bond, split(high))
        for n, k in enumerate(which):
            send_down[e, k] = high[:, n * sb:(n + 1) * sb]

        @pl.when(sec > 0)
        def _():
            down_copy(e).start()

    def local_part(src):
        right = split(right_ref[...])
        left = split(left_ref[...])
        group = 4

        for g in range(nph // group):
            block = src[pl.ds(g * group, group)].reshape(group * sb, sb)
            inner = dot3(split(block), right)
            inner = jnp.concatenate([inner[k * sb:(k + 1) * sb] for k in range(group)], axis=1)
            inner = dot3(left, split(inner))
            for k in range(group):
                loc_ref[g * group + k] = inner[:, k * sb:(k + 1) * sb]

        mats = split(mix_ref[...])
        step = 4
        for g in range(chunk_count // step):
            rows = pl.ds(g * (step * SUB), step * SUB)
            loc_ref[:, rows, :] += unlanes(dot3(mats, split(lanes(src[:, rows, :], step))), step)

    def await_components(e):
        @pl.when(sec > 0)
        def _():
            up_copy(e).wait_recv()

        @pl.when(sec < nsec - 1)
        def _():
            down_copy(e).wait_recv()

    def bond_product(e, count):
        low = jnp.concatenate([recv_low[e, k] for k in range(count)], axis=1)
        return dot3(split(coupt_ref[...]), split(low))

    def receive_components(e):
        await_components(e)
        low = bond_product(e, nhop)
        for k in range(nhop):
            low_ref[k] = low[:, k * sb:(k + 1) * sb]

    step = 2

    def over_chunks(e, ndots, update):
        mats = split(mixo_ref[...])
        sums = (jnp.zeros((SUB, sb), F32),) * ndots
        for g in range(chunk_count // step):
            rows = pl.ds(g * (step * SUB), step * SUB)
            both = jnp.concatenate(
                [lanes(low_ref[:, rows, :], step), lanes(recv_high[e, :, rows, :], step)], axis=0)
            hopping = unlanes(dot3(mats, split(both)), step)
            mask = chunk_mask(step * SUB, g * step * SUB)[None]
            image = (loc_ref[:, rows, :] + hopping) * mask
            sums = tuple(s + d for s, d in zip(sums, update(rows, image)))
        return sums

    def inner(a, b):
        prod = jnp.sum(a * b, axis=0)
        return jnp.sum(prod.reshape(step, SUB, sb), axis=0)

    def dot_copy(e, d):
        return pltpu.make_async_remote_copy(
            src_ref=dots_ref.at[e, sec], dst_ref=dots_ref.at[e, sec], send_sem=dot_send.at[e, d],
            recv_sem=dot_recv.at[e, d], device_id=at_sector(lax.rem(sec + d, nsec)), device_id_type=MESH)

    def send_dots(e, parts):
        for n, part in enumerate(parts):
            dots_ref[e, sec, n] = part
        for d in range(1, nsec):
            dot_copy(e, d).start()

    def receive_dots(e, ndots):
        for d in range(1, nsec):
            dot_copy(e, d).wait_recv()
        totals = []
        for n in range(ndots):
            total = dots_ref[e, 0, n]
            for q in range(1, nsec):
                total = total + dots_ref[e, q, n]
            totals.append(jnp.sum(jnp.sum(total, axis=1, keepdims=True), axis=0, keepdims=True))
        return totals

    for g in range(2):
        @pl.when(stays & (core == g))
        def _(g=g):
            pair_local().wait()

        @pl.when(jnp.logical_not(stays & (core == g)))
        def _(g=g):
            pair_remote(0, g).wait_recv()
    first, second = pair_ref[0], pair_ref[1]
    chain_ref[chip] = exact(first, second)

    def chain_copy(d):
        return pltpu.make_async_remote_copy(
            src_ref=chain_ref.at[chip], dst_ref=chain_ref.at[chip], send_sem=chain_send.at[d],
            recv_sem=chain_recv.at[d], device_id=at_chip(lax.rem(chip + d, nchip)), device_id_type=MESH)

    for d in range(1, nchip):
        chain_copy(d).start()

    for d in range(1, nchip):
        chain_copy(d).wait_recv()
    r_i = lax.broadcasted_iota(jnp.int32, (sb, sb), 0)
    c_i = lax.broadcasted_iota(jnp.int32, (sb, sb), 1)
    ident = jnp.where(r_i == c_i, 1.0, 0.0).astype(F32)
    left = ident
    right = jnp.where(side == 0, second, ident)
    for c in range(nchip - 1):
        block = jnp.where(c < chip, chain_ref[c], ident)
        left = block if c == 0 else exact(left, block)
        right = exact(right, jnp.where(c + 1 > chip, chain_ref[c + 1], ident))
    left = exact(left, jnp.where(side == 1, first, ident))
    left_ref[...] = exact(left.T, left)
    right_ref[...] = exact_nt(right, right)

    for n in (2, 1, 0):
        @pl.when(stays)
        def _(n=n):
            swap_local(n).wait()

        @pl.when(moved)
        def _(n=n):
            swap_remote(n).wait_recv()

    coupt_ref[...] = coupling_ref[...].T
    whole = chunk_mask(sb, 0)
    for p in range(nph):
        v_ref[p] = v_ref[p] * whole
    send_components(v_ref, 0)

    local_part(v_ref)
    receive_components(0)

    def start_update(rows, image):
        w_ref[:, rows, :] = image
        v = v_ref[:, rows, :]
        return inner(v, v), inner(v, image)

    send_dots(0, over_chunks(0, 2, start_update))
    send_components(w_ref, 1)
    local_part(w_ref)
    norm2, raw = receive_dots(0, 2)
    inv = 1.0 / jnp.sqrt(norm2 + EPSILON)
    rayleigh = raw * (inv * inv)
    receive_components(1)

    def first_update(rows, image):
        v = v_ref[:, rows, :] * inv
        w = w_ref[:, rows, :] * inv
        r = w - rayleigh * v
        u = image * inv - rayleigh * w
        v_ref[:, rows, :] = v
        w_ref[:, rows, :] = w
        r_ref[:, rows, :] = r
        u_ref[:, rows, :] = u
        return inner(r, r), inner(r, u), inner(v, u), inner(r, w)

    send_dots(1, over_chunks(1, 4, first_update))

    def ritz(sums, rayleigh):
        rr, ru, vu, rw = sums
        square = rr + EPSILON
        res_norm = jnp.sqrt(square)
        curvature = ru / square
        half_gap = 0.5 * (curvature - rayleigh)
        lowest = 0.5 * (rayleigh + curvature) - jnp.sqrt(half_gap * half_gap + square)
        second = lowest - rayleigh
        scale = jnp.sqrt(square + second * second)
        a = res_norm / scale
        b = second / (res_norm * scale)
        following = a * a * rayleigh + a * b * (vu + rw) + b * b * ru
        return lowest, a, b, following

    for it in range(ITERS - 2):
        e = it + 2
        send_components(u_ref, e)
        local_part(u_ref)
        _, a, b, following = ritz(receive_dots(e - 1, 4), rayleigh)
        receive_components(e)
        previous = rayleigh

        def step_update(rows, image, a=a, b=b, following=following, previous=previous):
            v = v_ref[:, rows, :]
            w = w_ref[:, rows, :]
            u = u_ref[:, rows, :]
            v_new = a * v + b * r_ref[:, rows, :]
            w_new = a * w + b * u
            r_new = w_new - following * v_new
            u_new = a * (u + previous * w) + b * image - following * w_new
            v_ref[:, rows, :] = v_new
            w_ref[:, rows, :] = w_new
            r_ref[:, rows, :] = r_new
            u_ref[:, rows, :] = u_new
            return inner(r_new, r_new), inner(r_new, u_new), inner(v_new, u_new), inner(r_new, w_new)

        send_dots(e, over_chunks(e, 4, step_update))
        rayleigh = following

    e = ITERS
    send_components(u_ref, e)
    local_part(u_ref)
    _, a, b, following = ritz(receive_dots(e - 1, 4), rayleigh)
    square = jnp.zeros((SUB, sb), F32)
    image_sum = jnp.zeros((SUB, sb), F32)
    for g in range(chunk_count // step):
        rows = pl.ds(g * (step * SUB), step * SUB)
        v = v_ref[:, rows, :]
        w = w_ref[:, rows, :]
        u = u_ref[:, rows, :]
        v_new = a * v + b * r_ref[:, rows, :]
        w_new = a * w + b * u
        r_new = w_new - following * v_new
        known = u + rayleigh * w
        v_ref[:, rows, :] = v_new
        r_ref[:, rows, :] = r_new
        square = square + inner(r_new, r_new)
        image_sum = image_sum + inner(r_new, a * known - following * w_new)
        image_sum = image_sum + b * inner(
            u, a * known + b * loc_ref[:, rows, :] - following * w_new)

    await_components(e)
    low = bond_product(e, hh)
    twice = jnp.zeros((sb, sb), F32)
    for k in range(hh):
        twice = twice + low[:, k * sb:(k + 1) * sb] * comp_ref[k]
    for k in range(hh, nhop):
        twice = twice + recv_high[e, k] * send_up[e, k]
    twice = jnp.sum(twice.reshape(chunk_count, SUB, sb), axis=0)
    send_dots(e, (square, image_sum + (2.0 * b * b) * twice))
    rr, ru = receive_dots(e, 2)
    zero = jnp.zeros((1, 1), F32)
    lowest, a, b, _ = ritz((rr, ru, zero, zero), following)
    energy_own[...] = jnp.broadcast_to(lowest, (SUB, sb))

    nout = 4
    per = nph // nout

    def out_local(n):
        part = pl.ds(n * per, per)
        return pltpu.make_async_copy(w_ref.at[part], out_ref.at[part], out_recv.at[n])

    def out_remote(n):
        part = pl.ds(n * per, per)
        return pltpu.make_async_remote_copy(
            src_ref=w_ref.at[part], dst_ref=out_ref.at[part], send_sem=out_send.at[n],
            recv_sem=out_recv.at[n], device_id=partner, device_id_type=MESH)

    def energy_remote():
        return pltpu.make_async_remote_copy(
            src_ref=energy_own, dst_ref=energy_got, send_sem=out_send.at[nout],
            recv_sem=out_recv.at[nout], device_id=partner, device_id_type=MESH)

    @pl.when(moved)
    def _():
        energy_remote().start()

    @pl.when(stays)
    def _():
        energy_got[...] = energy_own[...]

    for n in range(nout):
        for p in range(n * per, (n + 1) * per):
            w_ref[p] = a * v_ref[p] + b * r_ref[p]

        @pl.when(moved)
        def _(n=n):
            out_remote(n).start()

        @pl.when(stays)
        def _(n=n):
            out_local(n).start()

    @pl.when(moved)
    def _():
        energy_remote().wait()
        for n in range(nout):
            out_remote(n).wait()
        for n in range(3):
            swap_remote(n).wait_send()

    @pl.when(stays)
    def _():
        for n in range(nout):
            out_local(n).wait()

    energy_ref[...] = energy_got[0:1, 0:1]

    for k in range(2):
        @pl.when(jnp.logical_not(stays & (side == k)))
        def _(k=k):
            pair_remote(k, core).wait_send()

    for d in range(1, nchip):
        chain_copy(d).wait_send()
    for e in range(ITERS + 1):
        @pl.when(sec < nsec - 1)
        def _(e=e):
            up_copy(e).wait_send()

        @pl.when(sec > 0)
        def _(e=e):
            down_copy(e).wait_send()

        for d in range(1, nsec):
            dot_copy(e, d).wait_send()


def shards(nseg, nsec, psi_start, transfer, coupling, site_term, hop_out, hop_in, kept):
    _, _, nph, sb, _ = psi_start.shape
    nhop = hop_in.shape[0]
    rounds = ITERS + 1
    nchip = nseg // 2
    vmem = pl.BlockSpec(memory_space=pltpu.VMEM)
    anywhere = pl.BlockSpec(memory_space=pl.ANY)
    smem = pl.BlockSpec(memory_space=pltpu.SMEM)
    block = pltpu.VMEM((nph, sb, sb), F32)
    parts = pltpu.VMEM((nhop, sb, sb), F32)
    sent = pltpu.VMEM((rounds, nhop, sb, sb), F32)
    square = pltpu.VMEM((sb, sb), F32)
    tile = pltpu.VMEM((SUB, sb), F32)
    dma = pltpu.SemaphoreType.DMA
    psi, energy = pl.pallas_call(
        functools.partial(kernel, nseg, nsec),
        out_shape=(
            jax.ShapeDtypeStruct((nph, sb, sb), F32),
            jax.ShapeDtypeStruct((1, 1), F32),
        ),
        in_specs=[anywhere] * 3 + [vmem] * 3 + [smem],
        out_specs=(anywhere, vmem),
        scratch_shapes=[
            block, block, block, block, block, parts, parts,
            sent, sent, sent, sent,
            pltpu.VMEM((rounds, nsec, 4, SUB, sb), F32),
            pltpu.VMEM((2, sb, sb), F32), pltpu.VMEM((nchip, sb, sb), F32),
            square, square, square, square,
            pltpu.VMEM((2 * nhop, nph), F32), pltpu.VMEM((2 * nhop, nph), F32),
            pltpu.VMEM((nph * SUB, nph * SUB), F32),
            pltpu.VMEM((2 * nhop * SUB, nph * SUB), F32),
            pltpu.VMEM((nph * SUB, 2 * nhop * SUB), F32),
            tile, tile, tile, tile,
            dma((rounds,)), dma((rounds,)), dma((rounds,)), dma((rounds,)),
            dma((rounds, nsec)), dma((rounds, nsec)),
            dma((nchip,)), dma((nchip,)), dma((2,)), dma((2,)), dma((3,)), dma((3,)),
            dma((5,)), dma((5,)),
        ],
        compiler_params=pltpu.CompilerParams(
            collective_id=0, has_side_effects=True, vmem_limit_bytes=40 * 1024 * 1024
        ),
    )(psi_start[0, 0], transfer[0, 0], coupling[0], site_term, hop_out, hop_in, kept)
    return psi.reshape(psi_start.shape), energy.reshape(1)


def solution(mesh):
    placed = (
        P("seg", "sec", None, None, None),
        P("seg", "sec", None, None),
        P("sec", None, None),
        P(),
        P(),
        P(),
        P("seg", "sec"),
    )
    return jax.shard_map(
        functools.partial(shards, mesh.shape["seg"], mesh.shape["sec"]),
        mesh=mesh,
        in_specs=placed,
        out_specs=(P("seg", "sec", None, None, None), P("seg")),
        check_vma=False,
    )
```
